128 devices in a mesh: edp: 16 (over y, z_hi, core), ep: 8 (over x, z_lo).
Axes of the slice: x: 4, y: 4, z: 4 (z_hi: 2, z_lo: 2; z = z_hi * 2 + z_lo), core: 2. Of those that a mesh axis runs over, the one named last changes fastest.
Arguments:
- dense_input: bfloat16 [196608, 2048], P(('edp', 'ep')), may hold values from -24 to 24
- dense_cotangent: bfloat16 [196608, 1024], P(('edp', 'ep')), may hold values from -6 to 6
- expert_input: bfloat16 [8, 16384, 2048], P('ep', 'edp'), may hold values from -6 to 6
- expert_cotangent: bfloat16 [8, 16384, 768], P('ep', 'edp'), may hold values from -6 to 6
- dense_master: float32 [2048, 1024], P(('edp', 'ep')), may hold values from -0.125 to 0.125
- dense_first: float32 [2048, 1024], P(('edp', 'ep')), may hold values from -3 to 3
- dense_second: float32 [2048, 1024], P(('edp', 'ep')), may hold values from 0.01 to 1
- expert_master: float32 [8, 2048, 768], P('ep', 'edp'), may hold values from -0.125 to 0.125
- expert_first: float32 [8, 2048, 768], P('ep', 'edp'), may hold values from -3 to 3
- expert_second: float32 [8, 2048, 768], P('ep', 'edp'), may hold values from 0.01 to 1
Outputs:
- dense_param: float32 [2048, 1024], P(('edp', 'ep'))
- dense_first_new: float32 [2048, 1024], P(('edp', 'ep'))
- dense_second_new: float32 [2048, 1024], P(('edp', 'ep'))
- dense_weight: bfloat16 [2048, 1024], replicated
- expert_param: float32 [8, 2048, 768], P('ep', 'edp')
- expert_first_new: float32 [8, 2048, 768], P('ep', 'edp')
- expert_second_new: float32 [8, 2048, 768], P('ep', 'edp')
- expert_weight: bfloat16 [8, 2048, 768], P('ep')
The draws below stay inside these ranges and needn't reach their ends.
All inputs are finite; a program needn't handle non-finite values.
Results may differ from the reference program's by a relative error of at most 0.001.
Values may be sent and summed in bfloat16 or wider, within the bound.
No kernel may reach another device: no remote copies, remote signals or barrier semaphores. Data moves between devices by JAX's collectives and lax.ppermute only.
A program may use at most 128 MiB of HBM per device.

```python
import math
import jax
import jax.numpy as jnp
from jax import lax

D = 2048
FF = 768
KVW = 1024
EXPERTS = 8
STEP = 100
TOKENS = 196608
EROWS_ALL = 16384


def spiked(result, rng, source, target, blocks, factor):
    owner, partner = [(jnp.arange(result.shape[position]) // (result.shape[position] // blocks)).reshape([-1 if axis == position else 1 for axis in range(result.ndim)]) for position in (source, target)]
    chosen = jax.random.permutation(rng, blocks)[partner]
    strong = (owner == chosen) | (owner == (partner + blocks // 2) % blocks)
    return jnp.where(strong, factor * result, result)


def block_scale(own_key, shape, split, smallest, top_value):
    gain, own = 1.0, jax.random.fold_in(own_key, 6)
    for axis_at, blocks in split:
        heights = jnp.exp(jax.random.uniform(jax.random.fold_in(own, axis_at), (blocks,), jnp.float32, smallest / len(split), top_value / len(split)))
        gain = gain * jnp.repeat(heights, shape[axis_at] // blocks).reshape([-1 if axis == axis_at else 1 for axis in range(len(shape))])
    return gain


def centred(stream_key, extent, deviation, most, split=(), kind=jnp.bfloat16):
    gain = block_scale(stream_key, extent, split, -0.22, 0.18) if split else 1.0
    entries = jax.random.normal(stream_key, extent, jnp.float32) * deviation * gain
    return jnp.minimum(jnp.maximum(entries, -most), most).astype(kind)


def heavy_noise(stream_key, dims, spread, reach, pieces, heavy, held_as=jnp.bfloat16):
    entries = spread * jax.random.normal(stream_key, dims, jnp.float32)
    if pieces:
        entries = entries * block_scale(stream_key, dims, pieces, -0.22, 0.18)
    return jnp.clip(spiked(entries, jax.random.fold_in(stream_key, 3), *heavy), -reach, reach).astype(held_as)


def setup_inputs(seed: int = 0) -> dict:
    key_list = jax.random.split(jax.random.key(seed), 11)
    return {
        "dense_input": heavy_noise(key_list[0], (TOKENS, D), 1.0, 24.0, ((0, 128),), (0, 1, 128, 5.5)),
        "dense_cotangent": centred(key_list[1], (TOKENS, KVW), 1.0, 6.0, ((0, 128),)),
        "expert_input": heavy_noise(key_list[2], (EXPERTS, EROWS_ALL, D), 1.0, 6.0, ((0, 8), (1, 16)), (1, 2, 16, 2.0)),
        "expert_cotangent": centred(key_list[3], (EXPERTS, EROWS_ALL, FF), 1.0, 6.0, ((0, 8), (1, 16))),
        "dense_master": centred(key_list[4], (D, KVW), D ** -0.5, 0.125, ((0, 128),), jnp.float32),
        "dense_first": centred(key_list[5], (D, KVW), 0.3, 3.0, ((0, 128),), jnp.float32),
        "dense_second": jnp.clip(jnp.exp(math.log(1.0) - 4.6051702 * jax.random.uniform(key_list[6], (D, KVW), jnp.float32) ** block_scale(key_list[6], (D, KVW), ((0, 128),), -0.2, 0.2)), 0.01, 1.0),
        "expert_master": centred(key_list[7], (EXPERTS, D, FF), D ** -0.5, 0.125, ((0, 8), (1, 16)), jnp.float32),
        "expert_first": centred(key_list[8], (EXPERTS, D, FF), 0.3, 3.0, ((0, 8), (1, 16)), jnp.float32),
        "expert_second": jnp.clip(jnp.exp(math.log(1.0) - 4.6051702 * jax.random.uniform(key_list[9], (EXPERTS, D, FF), jnp.float32) ** block_scale(key_list[9], (EXPERTS, D, FF), ((0, 8), (1, 16)), -0.2, 0.2)), 0.01, 1.0),
    }


def adamw(param, first, second, grad, clip):
    scaled = clip * grad
    first_new = 0.9 * first + 0.1 * scaled
    second_new = 0.95 * second + 0.05 * scaled * scaled
    first_hat = first_new / (1.0 - 0.9 ** STEP)
    second_hat = second_new / (1.0 - 0.95 ** STEP)
    param_new = param - 0.001 * (first_hat / (jnp.sqrt(second_hat) + 1e-08) + 0.1 * param)
    return (param_new, first_new, second_new)

def reference(dense_input, dense_cotangent, expert_input, expert_cotangent, dense_master, dense_first, dense_second, expert_master, expert_first, expert_second):
    dense_grad = lax.dot_general(dense_input, dense_cotangent, (((0,), (0,)), ((), ())), preferred_element_type=jnp.float32)

    def one_expert(pair):
        return lax.dot_general(pair[0], pair[1], (((0,), (0,)), ((), ())), preferred_element_type=jnp.float32)
    expert_grad = lax.map(one_expert, (expert_input, expert_cotangent))
    total = jnp.sum(dense_grad * dense_grad) + jnp.sum(expert_grad * expert_grad)
    limit = 10.0 * math.sqrt(D * KVW + EXPERTS * D * FF)
    clip = jnp.minimum(1.0, limit / (jnp.sqrt(total) + 1e-06))
    dense_param, dense_first_new, dense_second_new = adamw(dense_master, dense_first, dense_second, dense_grad, clip)
    expert_param, expert_first_new, expert_second_new = adamw(expert_master, expert_first, expert_second, expert_grad, clip)
    return (dense_param, dense_first_new, dense_second_new, dense_param.astype(jnp.bfloat16), expert_param, expert_first_new, expert_second_new, expert_param.astype(jnp.bfloat16))
```

```python
import math

import jax
import jax.numpy as jnp
import numpy as np
from jax import lax
from jax.sharding import PartitionSpec as P

STEP = 100
BOTH = ("edp", "ep")
DIMS = (4, 2, 2, 4, 2)
f16, f32, bf16 = jnp.float16, jnp.float32, jnp.bfloat16


def pairs(move):
    out = []
    for src in range(math.prod(DIMS)):
        at = [int(v) for v in np.unravel_index(src, DIMS)]
        out.append((src, int(np.ravel_multi_index(move(*at), DIMS))))
    return out


def along(axis_of_core, k):
    def move(y, zh, c, x, zl):
        axis, z = axis_of_core[c], zh * 2 + zl
        if axis == "x":
            x = (x + k) % 4
        elif axis == "y":
            y = (y + k) % 4
        else:
            z = (z + k) % 4
        return y, z // 2, c, x, z % 2

    return pairs(move)


CORE = pairs(lambda y, zh, c, x, zl: (y, zh, 1 - c, x, zl))
ZHI = pairs(lambda y, zh, c, x, zl: (y, 1 - zh, c, x, zl))
FIRST = [along("xz", k) for k in range(4)]
SECOND = [along("zx", k) for k in range(4)]
YS = [along("yy", k) for k in range(4)]


def send(value, pairing):
    return lax.ppermute(value, BOTH, pairing)


def at(value, index, axis):
    return lax.dynamic_index_in_dim(value, index, axis, keepdims=False)


def ordered(pieces, own):
    ring = [pieces[0], pieces[3], pieces[2], pieces[1]]
    return lax.dynamic_slice_in_dim(jnp.stack(ring + ring), (4 - own) % 4, 4, 0)


def adamw(param, first, second, grad, clip):
    scaled = clip * grad
    first_new = 0.9 * first + 0.1 * scaled
    second_new = 0.95 * second + 0.05 * scaled * scaled
    first_hat = first_new / (1.0 - 0.9**STEP)
    second_hat = second_new / (1.0 - 0.95**STEP)
    param_new = param - 0.001 * (first_hat / (jnp.sqrt(second_hat) + 1e-08) + 0.1 * param)
    return (param_new, first_new, second_new)


def column_term(inputs, cotangent):
    return lax.dot_general(
        inputs, cotangent, (((0,), (0,)), ((), ())), preferred_element_type=jnp.float32
    )


def per_device(
    dense_input,
    dense_cotangent,
    expert_input,
    expert_cotangent,
    dense_master,
    dense_first,
    dense_second,
    expert_master,
    expert_first,
    expert_second,
):
    edp, ep = lax.axis_index("edp"), lax.axis_index("ep")
    y, zh, c, x, zl = edp // 4, (edp // 2) % 2, edp % 2, ep // 2, ep % 2
    z = zh * 2 + zl
    even = c == 0
    b, a = jnp.where(even, x, z), jnp.where(even, z, x)
    kvw, ff = dense_cotangent.shape[1], expert_cotangent.shape[2]
    rows = dense_master.shape[0]
    erows = expert_master.shape[1]

    g = (column_term(dense_input, dense_cotangent) * 0.25).astype(f16)
    g = g.reshape(4, 2, 2, 4, 2, rows, kvw)
    away = send(at(g, 1 - c, 2), CORE)
    q = column_term(expert_input[0], expert_cotangent[0]).astype(f16)
    q = q.reshape(4, 2, 2, erows, ff)
    eaway = send(at(q, 1 - c, 2), CORE)

    h = at(g, c, 2)

    def pick(value, k):
        byx = at(value, (x + k) % 4, 2).reshape(4, 4, rows, kvw)
        zk = (z + k) % 4
        byz = at(at(value, zk // 2, 1), zk % 2, 2)
        return jnp.where(even, byx, byz)

    def first_piece(k):
        return (pick(h, k).astype(f32) + pick(away, k).astype(f32)) * 0.5

    got = [send(first_piece(k).astype(f16), FIRST[k]) for k in (1, 2, 3)]
    qh = at(q, c, 2)

    def efirst_piece(k):
        yk = (y + k) % 4
        return (at(qh, yk, 0).astype(f32) + at(eaway, yk, 0).astype(f32)) * 0.5

    egot = [send(efirst_piece(k).astype(f16), YS[k]) for k in (1, 2, 3)]

    t = (first_piece(0) + sum(v.astype(f32) for v in got)) * 0.25
    got = [send(at(t, (a + k) % 4, 1).astype(f16), SECOND[k]) for k in (1, 2, 3)]
    et = (efirst_piece(0) + sum(v.astype(f32) for v in egot)) * 0.25
    egot = send(at(et, 1 - zh, 0).astype(f16), ZHI)
    u = at(t, a, 1) + sum(v.astype(f32) for v in got)
    got = [send(at(u, (y + k) % 4, 0), YS[k]) for k in (1, 2, 3)]
    expert_grad = ((at(et, zh, 0) + egot.astype(f32)) * 8.0)[None]
    dense_grad = (at(u, y, 0) + sum(got)) * 32.0

    mine = jnp.sum(dense_grad * dense_grad) + jnp.sum(expert_grad * expert_grad)
    spread = lax.all_to_all(jnp.full((128, 1, 128), mine, f32), BOTH, 0, 0, tiled=True)
    total = jnp.sum(spread[:, :, 0])
    ep_size = lax.axis_size("ep")
    limit = 10.0 * math.sqrt(dense_input.shape[1] * (kvw + ep_size * ff))
    clip = jnp.minimum(1.0, limit / (jnp.sqrt(total) + 1e-06))

    dense_param, dense_first_new, dense_second_new = adamw(
        dense_master, dense_first, dense_second, dense_grad, clip
    )
    expert_param, expert_first_new, expert_second_new = adamw(
        expert_master, expert_first, expert_second, expert_grad, clip
    )

    w = dense_param.astype(bf16)
    ew = expert_param.astype(bf16)[0]
    w = ordered([w] + [send(w, YS[k]) for k in (1, 2, 3)], y)
    eo = send(ew, ZHI)
    ew = jnp.where(zh == 0, jnp.stack([ew, eo]), jnp.stack([eo, ew]))
    w = ordered([w] + [send(w, SECOND[k]) for k in (1, 2, 3)], a)
    ew = ordered([ew] + [send(ew, YS[k]) for k in (1, 2, 3)], y)
    w = ordered([w] + [send(w, FIRST[k]) for k in (1, 2, 3)], b)
    eo = send(ew, CORE)
    wo = send(w, CORE)
    ew = jnp.where(even, jnp.stack([ew, eo], 2), jnp.stack([eo, ew], 2))
    w0 = jnp.where(even, w, wo).reshape(4, 2, 2, 4, rows, kvw).transpose(3, 1, 0, 2, 4, 5)
    w1 = jnp.where(even, wo, w).reshape(2, 2, 4, 4, rows, kvw).transpose(3, 0, 2, 1, 4, 5)
    dense_weight = jnp.stack([w0, w1], 2).reshape(-1, kvw)
    expert_weight = ew.reshape(1, -1, ff)
    return (
        dense_param,
        dense_first_new,
        dense_second_new,
        dense_weight,
        expert_param,
        expert_first_new,
        expert_second_new,
        expert_weight,
    )


def solution(mesh):
    placed = (
        P(BOTH, None),
        P(BOTH, None),
        P("ep", "edp", None),
        P("ep", "edp", None),
        P(BOTH, None),
        P(BOTH, None),
        P(BOTH, None),
        P("ep", "edp", None),
        P("ep", "edp", None),
        P("ep", "edp", None),
    )
    return jax.shard_map(
        per_device,
        mesh=mesh,
        in_specs=placed,
        out_specs=(
            P(BOTH, None),
            P(BOTH, None),
            P(BOTH, None),
            P(),
            P("ep", "edp", None),
            P("ep", "edp", None),
            P("ep", "edp", None),
            P("ep", None, None),
        ),
        check_vma=False,
    )
```

```python
import functools
import math

import jax
import jax.numpy as jnp
import numpy as np
from jax import lax
from jax.experimental import pallas as pl
from jax.experimental.pallas import tpu as pltpu
from jax.sharding import PartitionSpec as P

STEP = 100
VMEM = 24 * 1024 * 1024
BOTH = ("edp", "ep")
DIMS = (4, 2, 2, 4, 2)
LIGHT = pl.CostEstimate(flops=1, bytes_accessed=1, transcendentals=0)
f16, f32, bf16 = jnp.float16, jnp.float32, jnp.bfloat16


def pairs(move):
    out = []
    for src in range(math.prod(DIMS)):
        at = [int(v) for v in np.unravel_index(src, DIMS)]
        out.append((src, int(np.ravel_multi_index(move(*at), DIMS))))
    return out


def along(axis_of_core, k):
    def move(y, zh, c, x, zl):
        axis, z = axis_of_core[c], zh * 2 + zl
        if axis == "x":
            x = (x + k) % 4
        elif axis == "y":
            y = (y + k) % 4
        else:
            z = (z + k) % 4
        return y, z // 2, c, x, z % 2

    return pairs(move)


CORE = pairs(lambda y, zh, c, x, zl: (y, zh, 1 - c, x, zl))
ZHI = pairs(lambda y, zh, c, x, zl: (y, 1 - zh, c, x, zl))
FIRST = [along("xz", k) for k in range(4)]
SECOND = [along("zx", k) for k in range(4)]
YS = [along("yy", k) for k in range(4)]


def send(value, pairing):
    return lax.ppermute(value, BOTH, pairing)


def after(values, event):
    return lax.optimization_barrier((values, event))[0]


def ahead(own, received):
    return jnp.stack([own, received[2], received[1], received[0]])


def in_order(own, received, at):
    pieces = [own, *received]
    out = []
    for m in range(4):
        away = (at - m + 4) % 4
        out.append(jnp.where(away == 0, pieces[0], jnp.where(away == 1, pieces[1], jnp.where(away == 2, pieces[2], pieces[3]))))
    return jnp.stack(out)


def ring(value, pairings):
    return ahead(value, [send(value, p) for p in pairings[1:]])


def relative(pos, core, y, zh, x, zl):
    dx, dz, dy = (x - pos[3]) % 4, (zh * 2 + zl - pos[4]) % 4, (y - pos[0]) % 4
    even = core == 0
    return jnp.where(even, dx, dz), jnp.where(even, dz, dx), dy


def half_kernel(store, other, pos, inputs, cotangent, out, columns, held, sems):
    step = pl.program_id(0)
    core = (pos[2] + other) % 2
    width = columns.shape[2]

    def load(block):
        start = pl.multiple_of((2 * block + core) * width, width)
        return pltpu.make_async_copy(
            inputs.at[:, pl.ds(start, width)], columns.at[block], sems.at[block]
        )

    whole = pltpu.make_async_copy(cotangent, held, sems.at[8])

    @pl.when(step == 0)
    def _():
        whole.start()
        for block in range(8):
            load(block).start()
        whole.wait()

    for half in range(2):
        load(2 * step + half).wait()
    terms = column_term(
        jnp.concatenate([columns[2 * step], columns[2 * step + 1]], axis=1), held[...]
    )
    store(pos, core, step, terms, out)


def store_dense(pos, core, step, terms, out):
    rows = out.shape[3]
    for block in range(16):
        zh, x, zl = block // 8, block // 2 % 4, block % 2
        first, second, _ = relative(pos, core, step, zh, x, zl)
        out[first, second, 0] = terms[block * rows : (block + 1) * rows]


def store_expert(pos, core, step, terms, out):
    rows = out.shape[2]
    for zh in range(2):
        out[0, (zh + pos[1]) % 2] = terms[zh * rows : (zh + 1) * rows]


def half_terms(store, other, pos, inputs, cotangent, shape, block, at, name, vmem):
    depth, width = inputs.shape
    hbm = pl.BlockSpec(memory_space=pltpu.MemorySpace.HBM)
    return pl.pallas_call(
        functools.partial(half_kernel, store, other),
        out_shape=jax.ShapeDtypeStruct(shape, f32),
        grid_spec=pltpu.PrefetchScalarGridSpec(
            num_scalar_prefetch=1,
            grid=(4,),
            in_specs=[hbm, hbm],
            out_specs=pl.BlockSpec(block, at),
            scratch_shapes=[
                pltpu.VMEM((8, depth, width // 16), bf16),
                pltpu.VMEM(cotangent.shape, bf16),
                pltpu.SemaphoreType.DMA((9,)),
            ],
        ),
        compiler_params=pltpu.CompilerParams(vmem_limit_bytes=vmem),
        cost_estimate=pl.CostEstimate(
            flops=2 * depth * width * cotangent.shape[1], bytes_accessed=1, transcendentals=0
        ),
        name=name,
    )(pos, inputs, cotangent)


def dense_half(other, pos, inputs, cotangent):
    rows, kvw = inputs.shape[1] // 128, cotangent.shape[1]
    return half_terms(
        store_dense, other, pos, inputs, cotangent,
        (4, 4, 4, rows, kvw), (4, 4, 1, rows, kvw),
        lambda step, pos: (0, 0, (step - pos[0] + 4) % 4, 0, 0), "dense_terms",
        VMEM,
    )


def expert_half(other, pos, inputs, cotangent):
    rows, ff = inputs.shape[1] // 16, cotangent.shape[1]
    return half_terms(
        store_expert, other, pos, inputs, cotangent,
        (4, 2, rows, ff), (1, 2, rows, ff),
        lambda step, pos: ((step - pos[0] + 4) % 4, 0, 0, 0), "expert_terms",
        VMEM,
    )


def place_kernel(names, pos, *refs):
    pieces, (dense_out, expert_out, sems) = refs[: len(names)], refs[-3:]
    copies = []
    for (kind, other, first), piece in zip(names, pieces):
        core = (pos[2] + other) % 2
        even = core == 0
        if kind == "expert":
            for dy in range(4):
                for dz in range(2):
                    block = ((pos[0] + dy) % 4 * 2 + (pos[1] + dz) % 2) * 2 + core
                    copies.append((piece.at[dy, dz], expert_out.at[block]))
        else:
            for second in range(4):
                x = (pos[3] + jnp.where(even, first, second)) % 4
                z = (pos[4] + jnp.where(even, second, first)) % 4
                copies.append((piece.at[second], dense_out.at[:, z // 2, core, x, z % 2]))
    started = [pltpu.make_async_copy(*c, sems.at[i]) for i, c in enumerate(copies)]
    for copy in started:
        copy.start()
    for copy in started:
        copy.wait()


def place(pos, pieces, shapes, into=()):
    names = list(pieces)
    anywhere = pl.BlockSpec(memory_space=pl.ANY)
    count = sum(8 if n[0] == "expert" else 4 for n in names)
    return pl.pallas_call(
        functools.partial(place_kernel, names),
        out_shape=shapes,
        in_specs=[pl.BlockSpec(memory_space=pltpu.SMEM)]
        + [pl.BlockSpec(memory_space=pltpu.VMEM)] * len(names)
        + [anywhere] * len(into),
        out_specs=(anywhere, anywhere),
        scratch_shapes=[pltpu.SemaphoreType.DMA((count,))],
        input_output_aliases={1 + len(names) + i: i for i in range(len(into))},
        compiler_params=pltpu.CompilerParams(vmem_limit_bytes=VMEM),
        cost_estimate=LIGHT,
        name="place",
    )(pos, *pieces.values(), *into)


def adamw(param, first, second, grad, clip):
    scaled = clip * grad
    first_new = 0.9 * first + 0.1 * scaled
    second_new = 0.95 * second + 0.05 * scaled * scaled
    first_hat = first_new / (1.0 - 0.9**STEP)
    second_hat = second_new / (1.0 - 0.95**STEP)
    param_new = param - 0.001 * (first_hat / (jnp.sqrt(second_hat) + 1e-08) + 0.1 * param)
    return (param_new, first_new, second_new)


def column_term(inputs, cotangent):
    return lax.dot_general(
        inputs, cotangent, (((0,), (0,)), ((), ())), preferred_element_type=jnp.float32
    )


def per_device(
    dense_input,
    dense_cotangent,
    expert_input,
    expert_cotangent,
    dense_master,
    dense_first,
    dense_second,
    expert_master,
    expert_first,
    expert_second,
):
    edp, ep = lax.axis_index("edp"), lax.axis_index("ep")
    zh, zl = edp // 2 % 2, ep % 2
    pos = jnp.stack([edp // 4, zh, edp % 2, ep // 2, zh * 2 + zl]).astype(jnp.int32)
    kvw, ff = dense_cotangent.shape[1], expert_cotangent.shape[2]

    routed = expert_input[0], expert_cotangent[0]
    tokens = dense_input, dense_cotangent
    terms = expert_half(1, pos, *routed)
    eaway = send(terms, CORE)
    eown = expert_half(0, pos, *after(routed, terms))
    efirst = [eown[k] + eaway[k] for k in range(4)]
    epieces = [(efirst[k] * 0.5).astype(f16) for k in (1, 2, 3)]
    egot = [send(epieces[k - 1], YS[k]) for k in (1, 2, 3)]
    terms = dense_half(1, pos, *after(tokens, epieces))
    away = send(terms, CORE)
    own = dense_half(0, pos, *after(tokens, terms))
    first = [own[k] + away[k] for k in range(4)]
    pieces = [(first[k] * 0.125).astype(f16) for k in (1, 2, 3)]
    got = [send(pieces[k - 1], FIRST[k]) for k in (1, 2, 3)]
    egot = after(egot, pieces)
    esecond = efirst[0] * 0.5 + sum(v.astype(f32) for v in egot)
    egot = send((esecond[1] * 0.25).astype(f16), ZHI)
    second = first[0] * 0.125 + sum(v.astype(f32) for v in got)
    got = [send((second[k] * 0.25).astype(f16), SECOND[k]) for k in (1, 2, 3)]
    third = second[0] * 0.25 + sum(v.astype(f32) for v in got)
    got = [send(third[k], YS[k]) for k in (1, 2, 3)]
    expert_grad = ((esecond[0] * 0.25 + egot.astype(f32)) * 8.0)[None]
    dense_grad = (third[0] + sum(got)) * 32.0

    mine = jnp.sum(dense_grad * dense_grad) + jnp.sum(expert_grad * expert_grad)
    spread = lax.all_to_all(jnp.full((128, 1, 128), mine, f32), BOTH, 0, 0, tiled=True)
    total = jnp.sum(spread[:, :, 0])
    ep_size = lax.axis_size("ep")
    limit = 10.0 * math.sqrt(dense_input.shape[1] * (kvw + ep_size * ff))
    clip = jnp.minimum(1.0, limit / (jnp.sqrt(total) + 1e-06))

    dense_param, dense_first_new, dense_second_new = adamw(
        dense_master, dense_first, dense_second, dense_grad, clip
    )
    expert_param, expert_first_new, expert_second_new = adamw(
        expert_master, expert_first, expert_second, expert_grad, clip
    )

    w = dense_param.astype(bf16)
    w = in_order(w, [send(w, YS[k]) for k in (1, 2, 3)], edp // 4)
    ew = expert_param.astype(bf16)[0]
    ew = jnp.stack([ew, send(ew, ZHI)])
    w, ew = lax.optimization_barrier((w, ew))
    w, ew = lax.optimization_barrier((ring(w, SECOND), ring(ew, YS)))
    shapes = (
        jax.ShapeDtypeStruct(DIMS + w.shape[2:], bf16),
        jax.ShapeDtypeStruct((16,) + ew.shape[2:], bf16),
    )
    late = {("dense", 0, m): send(w, FIRST[4 - m]) for m in (1, 2, 3)}
    early = {("dense", 0, 0): w, ("dense", 1, 0): send(w, CORE)}
    early |= {("expert", 0, 0): ew, ("expert", 1, 0): send(ew, CORE)}
    placed = place(pos, early, shapes)
    late, placed = lax.optimization_barrier((list(late.values()), placed))
    late = {("dense", 0, m + 1): v for m, v in enumerate(late)}
    late |= {("dense", 1, m): send(v, CORE) for (_, _, m), v in late.items()}
    dense_weight, expert_weight = place(pos, late, shapes, placed)
    dense_weight = dense_weight.reshape(-1, kvw)
    expert_weight = expert_weight.reshape(1, -1, ff)
    return (
        dense_param,
        dense_first_new,
        dense_second_new,
        dense_weight,
        expert_param,
        expert_first_new,
        expert_second_new,
        expert_weight,
    )


def solution(mesh):
    placed = (
        P(BOTH, None),
        P(BOTH, None),
        P("ep", "edp", None),
        P("ep", "edp", None),
        P(BOTH, None),
        P(BOTH, None),
        P(BOTH, None),
        P("ep", "edp", None),
        P("ep", "edp", None),
        P("ep", "edp", None),
    )
    return jax.shard_map(
        per_device,
        mesh=mesh,
        in_specs=placed,
        out_specs=(
            P(BOTH, None),
            P(BOTH, None),
            P(BOTH, None),
            P(),
            P("ep", "edp", None),
            P("ep", "edp", None),
            P("ep", "edp", None),
            P("ep", None, None),
        ),
        check_vma=False,
    )
```

```python
import functools
import math

import jax
import jax.numpy as jnp
import numpy as np
from jax import lax
from jax.experimental import pallas as pl
from jax.experimental.pallas import tpu as pltpu
from jax.sharding import PartitionSpec as P

STEP = 100
VMEM = 24 * 1024 * 1024
BOTH = ("edp", "ep")
DIMS = (4, 2, 2, 4, 2)
LIGHT = pl.CostEstimate(flops=1, bytes_accessed=1, transcendentals=0)
f16, f32, bf16 = jnp.float16, jnp.float32, jnp.bfloat16


def pairs(move):
    out = []
    for src in range(math.prod(DIMS)):
        at = [int(v) for v in np.unravel_index(src, DIMS)]
        out.append((src, int(np.ravel_multi_index(move(*at), DIMS))))
    return out


def along(axis_of_core, k):
    def move(y, zh, c, x, zl):
        axis, z = axis_of_core[c], zh * 2 + zl
        if axis == "x":
            x = (x + k) % 4
        elif axis == "y":
            y = (y + k) % 4
        else:
            z = (z + k) % 4
        return y, z // 2, c, x, z % 2

    return pairs(move)


CORE = pairs(lambda y, zh, c, x, zl: (y, zh, 1 - c, x, zl))
ZHI = pairs(lambda y, zh, c, x, zl: (y, 1 - zh, c, x, zl))
FIRST = [along("xz", k) for k in range(4)]
SECOND = [along("zx", k) for k in range(4)]
YS = [along("yy", k) for k in range(4)]


def send(value, pairing):
    return lax.ppermute(value, BOTH, pairing)


def after(values, event):
    return lax.optimization_barrier((values, event))[0]


def ahead(own, received):
    return jnp.stack([own, received[2], received[1], received[0]])


def in_order(own, received, at):
    pieces = [own, *received]
    out = []
    for m in range(4):
        away = (at - m + 4) % 4
        out.append(jnp.where(away == 0, pieces[0], jnp.where(away == 1, pieces[1], jnp.where(away == 2, pieces[2], pieces[3]))))
    return jnp.stack(out)


def ring(value, pairings):
    return ahead(value, [send(value, p) for p in pairings[1:]])


def relative(pos, core, y, zh, x, zl):
    dx, dz, dy = (x - pos[3]) % 4, (zh * 2 + zl - pos[4]) % 4, (y - pos[0]) % 4
    even = core == 0
    return jnp.where(even, dx, dz), jnp.where(even, dz, dx), dy


def half_kernel(store, other, pos, inputs, cotangent, out, columns, held, sems):
    step = pl.program_id(0)
    core = (pos[2] + other) % 2
    width = columns.shape[2]

    def load(block):
        start = pl.multiple_of((2 * block + core) * width, width)
        return pltpu.make_async_copy(
            inputs.at[:, pl.ds(start, width)], columns.at[block], sems.at[block]
        )

    whole = pltpu.make_async_copy(cotangent, held, sems.at[8])

    @pl.when(step == 0)
    def _():
        whole.start()
        for block in range(8):
            load(block).start()
        whole.wait()

    for half in range(2):
        load(2 * step + half).wait()
    terms = column_term(
        jnp.concatenate([columns[2 * step], columns[2 * step + 1]], axis=1), held[...]
    )
    store(pos, core, step, terms, out)


def store_dense(pos, core, step, terms, out):
    rows = out.shape[3]
    for block in range(16):
        zh, x, zl = block // 8, block // 2 % 4, block % 2
        first, second, _ = relative(pos, core, step, zh, x, zl)
        out[first, second, 0] = terms[block * rows : (block + 1) * rows]


def store_expert(pos, core, step, terms, out):
    rows = out.shape[2]
    for zh in range(2):
        out[0, (zh + pos[1]) % 2] = terms[zh * rows : (zh + 1) * rows]


def half_terms(store, other, pos, inputs, cotangent, shape, block, at, name, vmem):
    depth, width = inputs.shape
    hbm = pl.BlockSpec(memory_space=pltpu.MemorySpace.HBM)
    return pl.pallas_call(
        functools.partial(half_kernel, store, other),
        out_shape=jax.ShapeDtypeStruct(shape, f32),
        grid_spec=pltpu.PrefetchScalarGridSpec(
            num_scalar_prefetch=1,
            grid=(4,),
            in_specs=[hbm, hbm],
            out_specs=pl.BlockSpec(block, at),
            scratch_shapes=[
                pltpu.VMEM((8, depth, width // 16), bf16),
                pltpu.VMEM(cotangent.shape, bf16),
                pltpu.SemaphoreType.DMA((9,)),
            ],
        ),
        compiler_params=pltpu.CompilerParams(vmem_limit_bytes=vmem),
        cost_estimate=pl.CostEstimate(
            flops=2 * depth * width * cotangent.shape[1], bytes_accessed=1, transcendentals=0
        ),
        name=name,
    )(pos, inputs, cotangent)


def dense_half(other, pos, inputs, cotangent):
    rows, kvw = inputs.shape[1] // 128, cotangent.shape[1]
    return half_terms(
        store_dense, other, pos, inputs, cotangent,
        (4, 4, 4, rows, kvw), (4, 4, 1, rows, kvw),
        lambda step, pos: (0, 0, (step - pos[0] + 4) % 4, 0, 0), "dense_terms",
        VMEM,
    )


def expert_half(other, pos, inputs, cotangent):
    rows, ff = inputs.shape[1] // 16, cotangent.shape[1]
    return half_terms(
        store_expert, other, pos, inputs, cotangent,
        (4, 2, rows, ff), (1, 2, rows, ff),
        lambda step, pos: ((step - pos[0] + 4) % 4, 0, 0, 0), "expert_terms",
        VMEM,
    )


def place_kernel(names, pos, *refs):
    pieces, (dense_out, expert_out, sems) = refs[: len(names)], refs[-3:]
    copies = []
    for (kind, other, first), piece in zip(names, pieces):
        core = (pos[2] + other) % 2
        even = core == 0
        if kind == "expert":
            for n, dy in enumerate(first):
                for dz in range(2):
                    block = ((pos[0] + dy) % 4 * 2 + (pos[1] + dz) % 2) * 2 + core
                    copies.append((piece.at[n, dz], expert_out.at[block]))
        else:
            for second in range(4):
                x = (pos[3] + jnp.where(even, first, second)) % 4
                z = (pos[4] + jnp.where(even, second, first)) % 4
                copies.append((piece.at[second], dense_out.at[:, z // 2, core, x, z % 2]))
    started = [pltpu.make_async_copy(*c, sems.at[i]) for i, c in enumerate(copies)]
    for copy in started:
        copy.start()
    for copy in started:
        copy.wait()


def place(pos, pieces, shapes, into=()):
    names = list(pieces)
    anywhere = pl.BlockSpec(memory_space=pl.ANY)
    count = sum(2 * len(n[2]) if n[0] == "expert" else 4 for n in names)
    return pl.pallas_call(
        functools.partial(place_kernel, names),
        out_shape=shapes,
        in_specs=[pl.BlockSpec(memory_space=pltpu.SMEM)]
        + [pl.BlockSpec(memory_space=pltpu.VMEM)] * len(names)
        + [anywhere] * len(into),
        out_specs=(anywhere, anywhere),
        scratch_shapes=[pltpu.SemaphoreType.DMA((count,))],
        input_output_aliases={1 + len(names) + i: i for i in range(len(into))},
        compiler_params=pltpu.CompilerParams(vmem_limit_bytes=VMEM),
        cost_estimate=LIGHT,
        name="place",
    )(pos, *pieces.values(), *into)


def adamw(param, first, second, grad, clip):
    scaled = clip * grad
    first_new = 0.9 * first + 0.1 * scaled
    second_new = 0.95 * second + 0.05 * scaled * scaled
    first_hat = first_new / (1.0 - 0.9**STEP)
    second_hat = second_new / (1.0 - 0.95**STEP)
    param_new = param - 0.001 * (first_hat / (jnp.sqrt(second_hat) + 1e-08) + 0.1 * param)
    return (param_new, first_new, second_new)


def column_term(inputs, cotangent):
    return lax.dot_general(
        inputs, cotangent, (((0,), (0,)), ((), ())), preferred_element_type=jnp.float32
    )


def per_device(
    dense_input,
    dense_cotangent,
    expert_input,
    expert_cotangent,
    dense_master,
    dense_first,
    dense_second,
    expert_master,
    expert_first,
    expert_second,
):
    edp, ep = lax.axis_index("edp"), lax.axis_index("ep")
    zh, zl = edp // 2 % 2, ep % 2
    pos = jnp.stack([edp // 4, zh, edp % 2, ep // 2, zh * 2 + zl]).astype(jnp.int32)
    kvw, ff = dense_cotangent.shape[1], expert_cotangent.shape[2]

    routed = expert_input[0], expert_cotangent[0]
    tokens = dense_input, dense_cotangent
    terms = expert_half(1, pos, *routed)
    eaway = send(terms, CORE)
    eown = expert_half(0, pos, *after(routed, terms))
    efirst = [eown[k] + eaway[k] for k in range(4)]
    epieces = [(efirst[k] * 0.5).astype(f16) for k in (1, 2, 3)]
    egot = [send(epieces[k - 1], YS[k]) for k in (1, 2, 3)]
    terms = dense_half(1, pos, *after(tokens, epieces))
    away = send(terms, CORE)
    own = dense_half(0, pos, *after(tokens, terms))
    first = [own[k] + away[k] for k in range(4)]
    pieces = [(first[k] * 0.125).astype(f16) for k in (1, 2, 3)]
    got = [send(pieces[k - 1], FIRST[k]) for k in (1, 2, 3)]
    egot = after(egot, pieces)
    esecond = efirst[0] * 0.5 + sum(v.astype(f32) for v in egot)
    egot = send((esecond[1] * 0.25).astype(f16), ZHI)
    second = first[0] * 0.125 + sum(v.astype(f32) for v in got)
    got = [send((second[k] * 0.25).astype(f16), SECOND[k]) for k in (1, 2, 3)]
    third = second[0] * 0.25 + sum(v.astype(f32) for v in got)
    got = [send(third[k], YS[k]) for k in (1, 2, 3)]
    expert_grad = ((esecond[0] * 0.25 + egot.astype(f32)) * 8.0)[None]
    dense_grad = (third[0] + sum(got)) * 32.0

    mine = jnp.sum(dense_grad * dense_grad) + jnp.sum(expert_grad * expert_grad)
    spread = lax.all_to_all(jnp.full((128, 1, 128), mine, f32), BOTH, 0, 0, tiled=True)
    total = jnp.sum(spread[:, :, 0])
    ep_size = lax.axis_size("ep")
    limit = 10.0 * math.sqrt(dense_input.shape[1] * (kvw + ep_size * ff))
    clip = jnp.minimum(1.0, limit / (jnp.sqrt(total) + 1e-06))

    dense_param, dense_first_new, dense_second_new = adamw(
        dense_master, dense_first, dense_second, dense_grad, clip
    )
    expert_param, expert_first_new, expert_second_new = adamw(
        expert_master, expert_first, expert_second, expert_grad, clip
    )

    w = dense_param.astype(bf16)
    ew = expert_param.astype(bf16)[0]
    w, ew = lax.optimization_barrier((w, ew))
    got = [send(w, YS[k]) for k in (1, 2, 3)], send(ew, ZHI)
    got, other = lax.optimization_barrier(got)
    w = in_order(w, got, edp // 4)
    ew = jnp.stack([ew, other])
    w, near = lax.optimization_barrier((ring(w, SECOND), [send(ew, YS[3]), send(ew, YS[1])]))
    far = send(ew, YS[2])[None]
    near = jnp.stack([ew, *near])
    shapes = (
        jax.ShapeDtypeStruct(DIMS + w.shape[2:], bf16),
        jax.ShapeDtypeStruct((16,) + ew.shape[1:], bf16),
    )
    late = [send(w, FIRST[4 - m]) for m in (1, 2, 3)]
    early = {("dense", 0, 0): w, ("dense", 1, 0): send(w, CORE)}
    early |= {("expert", 0, (0, 1, 3)): near, ("expert", 1, (0, 1, 3)): send(near, CORE)}
    placed = place(pos, early, shapes)
    late, far, placed = lax.optimization_barrier((late, far, placed))
    late = {("dense", 0, m + 1): v for m, v in enumerate(late)} | {("expert", 0, (2,)): far}
    swaps = {(d, 1, m): send(v, CORE) for (d, _, m), v in late.items()}
    placed = place(pos, late, shapes, placed)
    dense_weight, expert_weight = place(pos, swaps, shapes, placed)
    dense_weight = dense_weight.reshape(-1, kvw)
    expert_weight = expert_weight.reshape(1, -1, ff)
    return (
        dense_param,
        dense_first_new,
        dense_second_new,
        dense_weight,
        expert_param,
        expert_first_new,
        expert_second_new,
        expert_weight,
    )


def solution(mesh):
    placed = (
        P(BOTH, None),
        P(BOTH, None),
        P("ep", "edp", None),
        P("ep", "edp", None),
        P(BOTH, None),
        P(BOTH, None),
        P(BOTH, None),
        P("ep", "edp", None),
        P("ep", "edp", None),
        P("ep", "edp", None),
    )
    return jax.shard_map(
        per_device,
        mesh=mesh,
        in_specs=placed,
        out_specs=(
            P(BOTH, None),
            P(BOTH, None),
            P(BOTH, None),
            P(),
            P("ep", "edp", None),
            P("ep", "edp", None),
            P("ep", "edp", None),
            P("ep", None, None),
        ),
        check_vma=False,
    )
```

```python
import functools
import math

import jax
import jax.numpy as jnp
import numpy as np
from jax import lax
from jax.experimental import pallas as pl
from jax.experimental.pallas import tpu as pltpu
from jax.sharding import PartitionSpec as P

STEP = 100
VMEM = 24 * 1024 * 1024
BOTH = ("edp", "ep")
DIMS = (4, 2, 2, 4, 2)
LIGHT = pl.CostEstimate(flops=1, bytes_accessed=1, transcendentals=0)
f16, f32, bf16 = jnp.float16, jnp.float32, jnp.bfloat16


def pairs(move):
    out = []
    for src in range(math.prod(DIMS)):
        at = [int(v) for v in np.unravel_index(src, DIMS)]
        out.append((src, int(np.ravel_multi_index(move(*at), DIMS))))
    return out


def along(axis_of_core, k):
    def move(y, zh, c, x, zl):
        axis, z = axis_of_core[c], zh * 2 + zl
        if axis == "x":
            x = (x + k) % 4
        elif axis == "y":
            y = (y + k) % 4
        else:
            z = (z + k) % 4
        return y, z // 2, c, x, z % 2

    return pairs(move)


CORE = pairs(lambda y, zh, c, x, zl: (y, zh, 1 - c, x, zl))
ZHI = pairs(lambda y, zh, c, x, zl: (y, 1 - zh, c, x, zl))
FIRST = [along("xz", k) for k in range(4)]
SECOND = [along("zx", k) for k in range(4)]
YS = [along("yy", k) for k in range(4)]


def send(value, pairing):
    return lax.ppermute(value, BOTH, pairing)


def after(values, event):
    return lax.optimization_barrier((values, event))[0]


def ahead(own, received):
    return jnp.stack([own, received[2], received[1], received[0]])


def in_order(own, received, at):
    pieces = [own, *received]
    out = []
    for m in range(4):
        away = (at - m + 4) % 4
        out.append(jnp.where(away == 0, pieces[0], jnp.where(away == 1, pieces[1], jnp.where(away == 2, pieces[2], pieces[3]))))
    return jnp.stack(out)


def ring(value, pairings):
    return ahead(value, [send(value, p) for p in pairings[1:]])


def relative(pos, core, y, zh, x, zl):
    dx, dz, dy = (x - pos[3]) % 4, (zh * 2 + zl - pos[4]) % 4, (y - pos[0]) % 4
    even = core == 0
    return jnp.where(even, dx, dz), jnp.where(even, dz, dx), dy


def half_kernel(store, other, pos, inputs, cotangent, out, columns, held, sems):
    step = pl.program_id(0)
    core = (pos[2] + other) % 2
    width = columns.shape[2]

    def load(block):
        start = pl.multiple_of((2 * block + core) * width, width)
        return pltpu.make_async_copy(
            inputs.at[:, pl.ds(start, width)], columns.at[block], sems.at[block]
        )

    whole = pltpu.make_async_copy(cotangent, held, sems.at[8])

    @pl.when(step == 0)
    def _():
        whole.start()
        for block in range(8):
            load(block).start()
        whole.wait()

    for half in range(2):
        load(2 * step + half).wait()
    terms = column_term(
        jnp.concatenate([columns[2 * step], columns[2 * step + 1]], axis=1), held[...]
    )
    store(pos, core, step, terms, out)


def store_dense(pos, core, step, terms, out):
    rows = out.shape[3]
    for block in range(16):
        zh, x, zl = block // 8, block // 2 % 4, block % 2
        first, second, _ = relative(pos, core, step, zh, x, zl)
        out[first, second, 0] = terms[block * rows : (block + 1) * rows]


def store_expert(pos, core, step, terms, out):
    rows = out.shape[2]
    for zh in range(2):
        out[0, (zh + pos[1]) % 2] = terms[zh * rows : (zh + 1) * rows]


def half_terms(store, other, pos, inputs, cotangent, shape, block, at, name, vmem):
    depth, width = inputs.shape
    hbm = pl.BlockSpec(memory_space=pltpu.MemorySpace.HBM)
    return pl.pallas_call(
        functools.partial(half_kernel, store, other),
        out_shape=jax.ShapeDtypeStruct(shape, f32),
        grid_spec=pltpu.PrefetchScalarGridSpec(
            num_scalar_prefetch=1,
            grid=(4,),
            in_specs=[hbm, hbm],
            out_specs=pl.BlockSpec(block, at),
            scratch_shapes=[
                pltpu.VMEM((8, depth, width // 16), bf16),
                pltpu.VMEM(cotangent.shape, bf16),
                pltpu.SemaphoreType.DMA((9,)),
            ],
        ),
        compiler_params=pltpu.CompilerParams(vmem_limit_bytes=vmem),
        cost_estimate=pl.CostEstimate(
            flops=2 * depth * width * cotangent.shape[1], bytes_accessed=1, transcendentals=0
        ),
        name=name,
    )(pos, inputs, cotangent)


def dense_half(other, pos, inputs, cotangent):
    rows, kvw = inputs.shape[1] // 128, cotangent.shape[1]
    return half_terms(
        store_dense, other, pos, inputs, cotangent,
        (4, 4, 4, rows, kvw), (4, 4, 1, rows, kvw),
        lambda step, pos: (0, 0, (step - pos[0] + 4) % 4, 0, 0), "dense_terms",
        VMEM,
    )


def expert_half(other, pos, inputs, cotangent):
    rows, ff = inputs.shape[1] // 16, cotangent.shape[1]
    return half_terms(
        store_expert, other, pos, inputs, cotangent,
        (4, 2, rows, ff), (1, 2, rows, ff),
        lambda step, pos: ((step - pos[0] + 4) % 4, 0, 0, 0), "expert_terms",
        VMEM,
    )


def place_kernel(names, pos, *refs):
    pieces, (dense_out, expert_out, sems) = refs[: len(names)], refs[-3:]
    copies = []
    for (kind, other, first), piece in zip(names, pieces):
        core = (pos[2] + other) % 2
        even = core == 0
        if kind == "expert":
            for n, dy in enumerate(first):
                for dz in range(2):
                    block = ((pos[0] + dy) % 4 * 2 + (pos[1] + dz) % 2) * 2 + core
                    copies.append((piece.at[n, dz], expert_out.at[block]))
        else:
            for second in range(4):
                x = (pos[3] + jnp.where(even, first, second)) % 4
                z = (pos[4] + jnp.where(even, second, first)) % 4
                copies.append((piece.at[second], dense_out.at[:, z // 2, core, x, z % 2]))
    started = [pltpu.make_async_copy(*c, sems.at[i]) for i, c in enumerate(copies)]
    for copy in started:
        copy.start()
    for copy in started:
        copy.wait()


def place(pos, pieces, shapes, into=()):
    names = list(pieces)
    anywhere = pl.BlockSpec(memory_space=pl.ANY)
    count = sum(2 * len(n[2]) if n[0] == "expert" else 4 for n in names)
    return pl.pallas_call(
        functools.partial(place_kernel, names),
        out_shape=shapes,
        in_specs=[pl.BlockSpec(memory_space=pltpu.SMEM)]
        + [pl.BlockSpec(memory_space=pltpu.VMEM)] * len(names)
        + [anywhere] * len(into),
        out_specs=(anywhere, anywhere),
        scratch_shapes=[pltpu.SemaphoreType.DMA((count,))],
        input_output_aliases={1 + len(names) + i: i for i in range(len(into))},
        compiler_params=pltpu.CompilerParams(vmem_limit_bytes=VMEM),
        cost_estimate=LIGHT,
        name="place",
    )(pos, *pieces.values(), *into)


def adamw(param, first, second, grad, clip):
    scaled = clip * grad
    first_new = 0.9 * first + 0.1 * scaled
    second_new = 0.95 * second + 0.05 * scaled * scaled
    first_hat = first_new / (1.0 - 0.9**STEP)
    second_hat = second_new / (1.0 - 0.95**STEP)
    param_new = param - 0.001 * (first_hat / (jnp.sqrt(second_hat) + 1e-08) + 0.1 * param)
    return (param_new, first_new, second_new)


def lane_sums(value):
    parts = [value[:, at : at + 128] for at in range(0, value.shape[1], 128)]
    return jnp.sum(sum(v * v for v in parts), axis=0)


def column_term(inputs, cotangent):
    return lax.dot_general(
        inputs, cotangent, (((0,), (0,)), ((), ())), preferred_element_type=jnp.float32
    )


def per_device(
    dense_input,
    dense_cotangent,
    expert_input,
    expert_cotangent,
    dense_master,
    dense_first,
    dense_second,
    expert_master,
    expert_first,
    expert_second,
):
    edp, ep = lax.axis_index("edp"), lax.axis_index("ep")
    zh, zl = edp // 2 % 2, ep % 2
    pos = jnp.stack([edp // 4, zh, edp % 2, ep // 2, zh * 2 + zl]).astype(jnp.int32)
    kvw, ff = dense_cotangent.shape[1], expert_cotangent.shape[2]

    routed = expert_input[0], expert_cotangent[0]
    tokens = dense_input, dense_cotangent
    terms = expert_half(1, pos, *routed)
    eaway = send(terms, CORE)
    eown = expert_half(0, pos, *after(routed, terms))
    efirst = [eown[k] + eaway[k] for k in range(4)]
    epieces = [(efirst[k] * 0.5).astype(f16) for k in (1, 2, 3)]
    egot = [send(epieces[k - 1], YS[k]) for k in (1, 2, 3)]
    terms = dense_half(1, pos, *after(tokens, epieces))
    away = send(terms, CORE)
    own = dense_half(0, pos, *after(tokens, terms))
    first = [own[k] + away[k] for k in range(4)]
    pieces = [(first[k] * 0.125).astype(f16) for k in (1, 2, 3)]
    got = [send(pieces[k - 1], FIRST[k]) for k in (1, 3, 2)]
    egot = after(egot, pieces)
    esecond = efirst[0] * 0.5 + sum(v.astype(f32) for v in egot)
    egot = send((esecond[1] * 0.25).astype(f16), ZHI)
    second = first[0] * 0.125 + sum(v.astype(f32) for v in got)
    got = [send((second[k] * 0.25).astype(f16), SECOND[k]) for k in (1, 2, 3)]
    third = second[0] * 0.25 + sum(v.astype(f32) for v in got)
    got = [send(third[k], YS[k]) for k in (1, 2, 3)]
    expert_grad = ((esecond[0] * 0.25 + egot.astype(f32)) * 8.0)[None]
    dense_grad = (third[0] + sum(got)) * 32.0

    mine = lane_sums(dense_grad) + lane_sums(expert_grad[0])
    spread = jnp.broadcast_to(mine, (128, 1, 128))
    total = jnp.sum(lax.all_to_all(spread, BOTH, 0, 0, tiled=True))
    ep_size = lax.axis_size("ep")
    limit = 10.0 * math.sqrt(dense_input.shape[1] * (kvw + ep_size * ff))
    clip = jnp.minimum(1.0, limit / (jnp.sqrt(total) + 1e-06))

    dense_param, dense_first_new, dense_second_new = adamw(
        dense_master, dense_first, dense_second, dense_grad, clip
    )
    expert_param, expert_first_new, expert_second_new = adamw(
        expert_master, expert_first, expert_second, expert_grad, clip
    )

    w = dense_param.astype(bf16)
    ew = expert_param.astype(bf16)[0]
    w, ew = lax.optimization_barrier((w, ew))
    got = [send(w, YS[k]) for k in (1, 2, 3)], send(ew, ZHI)
    got, other = lax.optimization_barrier(got)
    w = in_order(w, got, edp // 4)
    ew = jnp.stack([ew, other])
    w, near = lax.optimization_barrier((ring(w, SECOND), [send(ew, YS[3]), send(ew, YS[1])]))
    far = send(ew, YS[2])[None]
    near = jnp.stack([ew, *near])
    shapes = (
        jax.ShapeDtypeStruct(DIMS + w.shape[2:], bf16),
        jax.ShapeDtypeStruct((16,) + ew.shape[1:], bf16),
    )
    late = [send(w, FIRST[4 - m]) for m in (1, 2, 3)]
    early = {("dense", 0, 0): w, ("dense", 1, 0): send(w, CORE)}
    early |= {("expert", 0, (0, 1, 3)): near, ("expert", 1, (0, 1, 3)): send(near, CORE)}
    placed = place(pos, early, shapes)
    late, far, placed = lax.optimization_barrier((late, far, placed))
    late = {("dense", 0, m + 1): v for m, v in enumerate(late)} | {("expert", 0, (2,)): far}
    swaps = {(d, 1, m): send(v, CORE) for (d, _, m), v in late.items()}
    placed = place(pos, late, shapes, placed)
    dense_weight, expert_weight = place(pos, swaps, shapes, placed)
    dense_weight = dense_weight.reshape(-1, kvw)
    expert_weight = expert_weight.reshape(1, -1, ff)
    return (
        dense_param,
        dense_first_new,
        dense_second_new,
        dense_weight,
        expert_param,
        expert_first_new,
        expert_second_new,
        expert_weight,
    )


def solution(mesh):
    placed = (
        P(BOTH, None),
        P(BOTH, None),
        P("ep", "edp", None),
        P("ep", "edp", None),
        P(BOTH, None),
        P(BOTH, None),
        P(BOTH, None),
        P("ep", "edp", None),
        P("ep", "edp", None),
        P("ep", "edp", None),
    )
    return jax.shard_map(
        per_device,
        mesh=mesh,
        in_specs=placed,
        out_specs=(
            P(BOTH, None),
            P(BOTH, None),
            P(BOTH, None),
            P(),
            P("ep", "edp", None),
            P("ep", "edp", None),
            P("ep", "edp", None),
            P("ep", None, None),
        ),
        check_vma=False,
    )
```

```python
import functools
import math

import jax
import jax.numpy as jnp
import numpy as np
from jax import lax
from jax.experimental import pallas as pl
from jax.experimental.pallas import tpu as pltpu
from jax.sharding import PartitionSpec as P

STEP = 100
VMEM = 24 * 1024 * 1024
BOTH = ("edp", "ep")
DIMS = (4, 2, 2, 4, 2)
LIGHT = pl.CostEstimate(flops=1, bytes_accessed=1, transcendentals=0)
f16, f32, bf16 = jnp.float16, jnp.float32, jnp.bfloat16


def pairs(move):
    out = []
    for src in range(math.prod(DIMS)):
        at = [int(v) for v in np.unravel_index(src, DIMS)]
        out.append((src, int(np.ravel_multi_index(move(*at), DIMS))))
    return out


def along(axis_of_core, k):
    def move(y, zh, c, x, zl):
        axis, z = axis_of_core[c], zh * 2 + zl
        if axis == "x":
            x = (x + k) % 4
        elif axis == "y":
            y = (y + k) % 4
        else:
            z = (z + k) % 4
        return y, z // 2, c, x, z % 2

    return pairs(move)


CORE = pairs(lambda y, zh, c, x, zl: (y, zh, 1 - c, x, zl))
ZHI = pairs(lambda y, zh, c, x, zl: (y, 1 - zh, c, x, zl))
FIRST = [along("xz", k) for k in range(4)]
SECOND = [along("zx", k) for k in range(4)]
YS = [along("yy", k) for k in range(4)]


def send(value, pairing):
    return lax.ppermute(value, BOTH, pairing)


def after(values, event):
    return lax.optimization_barrier((values, event))[0]


def ahead(own, received):
    return jnp.stack([own, received[2], received[1], received[0]])


def in_order(own, received, at):
    pieces = [own, *received]
    out = []
    for m in range(4):
        away = (at - m + 4) % 4
        out.append(jnp.where(away == 0, pieces[0], jnp.where(away == 1, pieces[1], jnp.where(away == 2, pieces[2], pieces[3]))))
    return jnp.stack(out)


def ring(value, pairings):
    return ahead(value, [send(value, p) for p in pairings[1:]])


def relative(pos, core, y, zh, x, zl):
    dx, dz, dy = (x - pos[3]) % 4, (zh * 2 + zl - pos[4]) % 4, (y - pos[0]) % 4
    even = core == 0
    return jnp.where(even, dx, dz), jnp.where(even, dz, dx), dy


def half_kernel(store, other, pos, inputs, cotangent, out, columns, held, sems):
    step = pl.program_id(0)
    core = (pos[2] + other) % 2
    width = columns.shape[2]

    def load(block):
        start = pl.multiple_of((2 * block + core) * width, width)
        return pltpu.make_async_copy(
            inputs.at[:, pl.ds(start, width)], columns.at[block], sems.at[block]
        )

    whole = pltpu.make_async_copy(cotangent, held, sems.at[8])

    @pl.when(step == 0)
    def _():
        whole.start()
        for block in range(8):
            load(block).start()
        whole.wait()

    for half in range(2):
        load(2 * step + half).wait()
    terms = column_term(
        jnp.concatenate([columns[2 * step], columns[2 * step + 1]], axis=1), held[...]
    )
    store(pos, core, step, terms, out)


def store_dense(pos, core, step, terms, out):
    rows = out.shape[3]
    for block in range(16):
        zh, x, zl = block // 8, block // 2 % 4, block % 2
        first, second, _ = relative(pos, core, step, zh, x, zl)
        out[first, second, 0] = terms[block * rows : (block + 1) * rows]


def store_expert(pos, core, step, terms, out):
    rows = out.shape[2]
    for zh in range(2):
        out[0, (zh + pos[1]) % 2] = terms[zh * rows : (zh + 1) * rows]


def half_terms(store, other, pos, inputs, cotangent, shape, block, at, name, vmem):
    depth, width = inputs.shape
    hbm = pl.BlockSpec(memory_space=pltpu.MemorySpace.HBM)
    return pl.pallas_call(
        functools.partial(half_kernel, store, other),
        out_shape=jax.ShapeDtypeStruct(shape, f32),
        grid_spec=pltpu.PrefetchScalarGridSpec(
            num_scalar_prefetch=1,
            grid=(4,),
            in_specs=[hbm, hbm],
            out_specs=pl.BlockSpec(block, at),
            scratch_shapes=[
                pltpu.VMEM((8, depth, width // 16), bf16),
                pltpu.VMEM(cotangent.shape, bf16),
                pltpu.SemaphoreType.DMA((9,)),
            ],
        ),
        compiler_params=pltpu.CompilerParams(vmem_limit_bytes=vmem),
        cost_estimate=pl.CostEstimate(
            flops=2 * depth * width * cotangent.shape[1], bytes_accessed=1, transcendentals=0
        ),
        name=name,
    )(pos, inputs, cotangent)


def dense_half(other, pos, inputs, cotangent):
    rows, kvw = inputs.shape[1] // 128, cotangent.shape[1]
    return half_terms(
        store_dense, other, pos, inputs, cotangent,
        (4, 4, 4, rows, kvw), (4, 4, 1, rows, kvw),
        lambda step, pos: (0, 0, (step - pos[0] + 4) % 4, 0, 0), "dense_terms",
        VMEM,
    )


def expert_half(other, pos, inputs, cotangent):
    rows, ff = inputs.shape[1] // 16, cotangent.shape[1]
    return half_terms(
        store_expert, other, pos, inputs, cotangent,
        (4, 2, rows, ff), (1, 2, rows, ff),
        lambda step, pos: ((step - pos[0] + 4) % 4, 0, 0, 0), "expert_terms",
        VMEM,
    )


def place_kernel(names, pos, *refs):
    pieces, (dense_out, expert_out, sems) = refs[: len(names)], refs[-3:]
    copies = []
    for (kind, other, first), piece in zip(names, pieces):
        core = (pos[2] + other) % 2
        even = core == 0
        if kind == "expert":
            for n, dy in enumerate(first):
                for dz in range(2):
                    block = ((pos[0] + dy) % 4 * 2 + (pos[1] + dz) % 2) * 2 + core
                    copies.append((piece.at[n, dz], expert_out.at[block]))
        else:
            for second in range(4):
                x = (pos[3] + jnp.where(even, first, second)) % 4
                z = (pos[4] + jnp.where(even, second, first)) % 4
                copies.append((piece.at[second], dense_out.at[:, z // 2, core, x, z % 2]))
    started = [pltpu.make_async_copy(*c, sems.at[i]) for i, c in enumerate(copies)]
    for copy in started:
        copy.start()
    for copy in started:
        copy.wait()


def place(pos, pieces, shapes, into=()):
    names = list(pieces)
    anywhere = pl.BlockSpec(memory_space=pl.ANY)
    count = sum(2 * len(n[2]) if n[0] == "expert" else 4 for n in names)
    return pl.pallas_call(
        functools.partial(place_kernel, names),
        out_shape=shapes,
        in_specs=[pl.BlockSpec(memory_space=pltpu.SMEM)]
        + [pl.BlockSpec(memory_space=pltpu.VMEM)] * len(names)
        + [anywhere] * len(into),
        out_specs=(anywhere, anywhere),
        scratch_shapes=[pltpu.SemaphoreType.DMA((count,))],
        input_output_aliases={1 + len(names) + i: i for i in range(len(into))},
        compiler_params=pltpu.CompilerParams(vmem_limit_bytes=VMEM),
        cost_estimate=LIGHT,
        name="place",
    )(pos, *pieces.values(), *into)


def adamw(param, first, second, grad, clip):
    scaled = clip * grad
    first_new = 0.9 * first + 0.1 * scaled
    second_new = 0.95 * second + 0.05 * scaled * scaled
    first_hat = first_new / (1.0 - 0.9**STEP)
    second_hat = second_new / (1.0 - 0.95**STEP)
    param_new = param - 0.001 * (first_hat / (jnp.sqrt(second_hat) + 1e-08) + 0.1 * param)
    return (param_new, first_new, second_new)


def lane_sums(value):
    parts = [value[:, at : at + 128] for at in range(0, value.shape[1], 128)]
    return jnp.sum(sum(v * v for v in parts), axis=0)


def column_term(inputs, cotangent):
    return lax.dot_general(
        inputs, cotangent, (((0,), (0,)), ((), ())), preferred_element_type=jnp.float32
    )


def per_device(
    dense_input,
    dense_cotangent,
    expert_input,
    expert_cotangent,
    dense_master,
    dense_first,
    dense_second,
    expert_master,
    expert_first,
    expert_second,
):
    edp, ep = lax.axis_index("edp"), lax.axis_index("ep")
    zh, zl = edp // 2 % 2, ep % 2
    pos = jnp.stack([edp // 4, zh, edp % 2, ep // 2, zh * 2 + zl]).astype(jnp.int32)
    kvw, ff = dense_cotangent.shape[1], expert_cotangent.shape[2]

    routed = expert_input[0], expert_cotangent[0]
    tokens = dense_input, dense_cotangent
    terms = expert_half(1, pos, *routed)
    eaway = send(terms, CORE)
    eown = expert_half(0, pos, *after(routed, terms))
    efirst = [eown[k] + eaway[k] for k in range(4)]
    epieces = [(efirst[k] * 0.5).astype(f16) for k in (1, 2, 3)]
    egot = [send(epieces[k - 1], YS[k]) for k in (1, 2, 3)]
    terms = dense_half(1, pos, *after(tokens, epieces))
    away = send(terms, CORE)
    own = dense_half(0, pos, *after(tokens, terms))
    first = [own[k] + away[k] for k in range(4)]
    pieces = [(first[k] * 0.125).astype(f16) for k in (1, 2, 3)]
    got = [send(pieces[k - 1], FIRST[k]) for k in (1, 3, 2)]
    egot = after(egot, pieces)
    esecond = efirst[0] * 0.5 + sum(v.astype(f32) for v in egot)
    egot = send((esecond[1] * 0.25).astype(f16), ZHI)
    second = first[0] * 0.125 + sum(v.astype(f32) for v in got)
    got = [send((second[k] * 0.25).astype(f16), SECOND[k]) for k in (1, 2, 3)]
    third = second[0] * 0.25 + sum(v.astype(f32) for v in got)
    got = [send(third[k], YS[k]) for k in (1, 2, 3)]
    expert_grad = ((esecond[0] * 0.25 + egot.astype(f32)) * 8.0)[None]
    dense_grad = (third[0] + sum(got)) * 32.0

    mine = lane_sums(dense_grad) + lane_sums(expert_grad[0])
    spread = jnp.broadcast_to(mine, (128, 1, 128))
    total = jnp.sum(lax.all_to_all(spread, BOTH, 0, 0, tiled=True))
    ep_size = lax.axis_size("ep")
    limit = 10.0 * math.sqrt(dense_input.shape[1] * (kvw + ep_size * ff))
    clip = jnp.minimum(1.0, limit / (jnp.sqrt(total) + 1e-06))

    dense_param, dense_first_new, dense_second_new = adamw(
        dense_master, dense_first, dense_second, dense_grad, clip
    )
    expert_param, expert_first_new, expert_second_new = adamw(
        expert_master, expert_first, expert_second, expert_grad, clip
    )

    w = dense_param.astype(bf16)
    ew = expert_param.astype(bf16)[0]
    w, ew = lax.optimization_barrier((w, ew))
    got = [send(w, YS[k]) for k in (1, 2, 3)], send(ew, ZHI)
    got, other = lax.optimization_barrier(got)
    w = in_order(w, got, edp // 4)
    ew = jnp.stack([ew, other])
    w, near = lax.optimization_barrier((ring(w, SECOND), [send(ew, YS[3]), send(ew, YS[1])]))
    far = send(ew, YS[2])[None]
    near = jnp.stack([ew, *near])
    shapes = (
        jax.ShapeDtypeStruct(DIMS + w.shape[2:], bf16),
        jax.ShapeDtypeStruct((16,) + ew.shape[1:], bf16),
    )
    late = [send(w, FIRST[4 - m]) for m in (1, 3, 2)]
    early = {("dense", 0, 0): w, ("dense", 1, 0): send(w, CORE)}
    early |= {("expert", 0, (0, 1, 3)): near, ("expert", 1, (0, 1, 3)): send(near, CORE)}
    placed = place(pos, early, shapes)
    late, far, placed = lax.optimization_barrier((late, far, placed))
    late = {("dense", 0, m): v for m, v in zip((1, 3, 2), late)} | {("expert", 0, (2,)): far}
    swaps = {(d, 1, m): send(v, CORE) for (d, _, m), v in late.items()}
    placed = place(pos, late, shapes, placed)
    dense_weight, expert_weight = place(pos, swaps, shapes, placed)
    dense_weight = dense_weight.reshape(-1, kvw)
    expert_weight = expert_weight.reshape(1, -1, ff)
    return (
        dense_param,
        dense_first_new,
        dense_second_new,
        dense_weight,
        expert_param,
        expert_first_new,
        expert_second_new,
        expert_weight,
    )


def solution(mesh):
    placed = (
        P(BOTH, None),
        P(BOTH, None),
        P("ep", "edp", None),
        P("ep", "edp", None),
        P(BOTH, None),
        P(BOTH, None),
        P(BOTH, None),
        P("ep", "edp", None),
        P("ep", "edp", None),
        P("ep", "edp", None),
    )
    return jax.shard_map(
        per_device,
        mesh=mesh,
        in_specs=placed,
        out_specs=(
            P(BOTH, None),
            P(BOTH, None),
            P(BOTH, None),
            P(),
            P("ep", "edp", None),
            P("ep", "edp", None),
            P("ep", "edp", None),
            P("ep", None, None),
        ),
        check_vma=False,
    )
```
